32 devices in a mesh: groups: 2 (over y), dp: 8 (over z, x), feat: 2 (over core).
Axes of the slice: x: 2, y: 2, z: 4, core: 2. Of those that a mesh axis runs over, the one named last changes fastest.
Arguments:
- frames: float32 [262144, 128], P(('groups', 'dp', 'feat')), parts along dimension 0, may hold values from -6 to 6
- pivots: int32 [4, 128], P('groups'), parts along dimension 0, may hold values from 0 to 131071, as said below
Outputs:
- factor: float32 [262144, 256], P(('groups', 'dp', 'feat')), parts along dimension 0
- residual_diag: float32 [262144], P(('groups', 'dp', 'feat')), parts along dimension 0
The draws below stay inside these ranges and needn't reach their ends.
There are 2 independent parts, one for each index of `groups`. The reference program is written for one: setup_inputs(seed, part) draws one part's arguments, and reference() takes and returns one part's arrays. A program takes and returns all parts, laid end to end along the dimension named above; each array names one. Nothing has to cross between parts.
Inputs may be any that keep to these rules, and one draw needn't show every extreme that they name: `pivots`: each row holds 128 distinct frame ids and no id is in both rows. Frame f lies on the device at index f // 8192 along dp+feat. At most 32 ids of one row lie on one device, and in every row some device holds exactly 32.
All inputs are finite; a program needn't handle non-finite values.
Results may differ from the reference program's by a relative error of at most 0.0003.
Values sent between devices are 32-bit elements; how exact they have to be, the bound alone decides.
A program may use at most 64 MiB of HBM per device.

```python
import jax
import jax.numpy as jnp
from jax import lax

FEAT = 128
BLOCK = 128
ROWS = 8192
FRAMES = 131072
MOST = 32


def draw_pivots(key, part):
    key = jax.random.fold_in(key, 11)
    devices = FRAMES // ROWS
    slot_total = devices * MOST
    block_rows = []
    for block_index in range(2):
        block_key = jax.random.fold_in(key, block_index)
        key_order, key_rest, key_shuffle, key_base = jax.random.split(block_key, 4)
        dev_order = jax.random.permutation(key_order, devices).astype(jnp.int32)
        rest_slots = jax.random.permutation(key_rest, slot_total - MOST)[:BLOCK - MOST].astype(jnp.int32) + MOST
        chosen = jnp.concatenate([jnp.arange(MOST, dtype=jnp.int32), rest_slots])
        chosen = jax.random.permutation(key_shuffle, chosen)
        base_rows = jax.random.randint(key_base, (devices,), 0, ROWS // (2 * MOST), dtype=jnp.int32)
        owner_dev = dev_order[chosen // MOST]
        frame_ids = owner_dev * ROWS + base_rows[owner_dev] * (2 * MOST) + block_index * MOST + chosen % MOST
        block_rows.append(frame_ids.astype(jnp.int32))
    return jnp.stack(block_rows, axis=0)


def levels(rng, dims, cuts, least, high):
    factor_of = 1.0
    for dim, blocks in cuts:
        heights = jax.random.uniform(jax.random.fold_in(jax.random.fold_in(rng, 6), dim), (blocks,), jnp.float32, least / len(cuts), high / len(cuts))
        factor_of = factor_of * jnp.repeat(jnp.exp(heights), dims[dim] // blocks).reshape((-1,) + (1,) * (len(dims) - 1 - dim))
    return factor_of


def normal_values(rng, extent, width, most, shards=(), held_as=jnp.bfloat16):
    values = jax.random.normal(rng, extent, jnp.float32) * width
    if len(shards) > 0:
        values = levels(rng, extent, shards, -0.22, 0.18) * values
    return jnp.clip(values, min=-most, max=most).astype(held_as)


def setup_inputs(seed: int = 0, part: int = 0) -> dict:
    key_list = jax.random.split(jax.random.key(seed), 3)
    part_keys = jax.random.split(jax.random.fold_in(key_list[2], part), 3)
    frames = normal_values(part_keys[0], (FRAMES, FEAT), 1.0, 6.0, ((0, 16),), jnp.float32)
    pivots = draw_pivots(jax.random.fold_in(jax.random.fold_in(key_list[2], part), 71), part)
    return {"frames": frames, "pivots": pivots}


def kernel_block(left, right):
    products = jnp.dot(left.astype(jnp.float32), right.T.astype(jnp.float32), precision=lax.Precision.HIGHEST, preferred_element_type=jnp.float32)
    left_sq = jnp.sum(left * left, axis=1)
    right_sq = jnp.sum(right * right, axis=1)
    distance = left_sq[:, None] + right_sq[None, :] - 2.0 * products
    return jnp.exp(distance * (-0.5 / FEAT))

def lower_inverse(pivot_block):
    lower_part = jnp.linalg.cholesky(pivot_block)
    identity = jnp.eye(pivot_block.shape[0], dtype=pivot_block.dtype)
    return jax.scipy.linalg.solve_triangular(lower_part, identity, lower=True)

def new_columns(columns, pivot_block):
    inverse = lower_inverse(pivot_block)
    return jnp.dot(columns.astype(jnp.float32), inverse.T.astype(jnp.float32), precision=lax.Precision.HIGHEST, preferred_element_type=jnp.float32)

def reference(frames, pivots):
    first_ids = pivots[0]
    second_ids = pivots[1]
    first_points = frames[first_ids]
    first_factor = new_columns(kernel_block(frames, first_points), kernel_block(first_points, first_points))
    second_points = frames[second_ids]
    earlier_rows = first_factor[second_ids]
    columns = kernel_block(frames, second_points) - jnp.dot(first_factor.astype(jnp.float32), earlier_rows.T.astype(jnp.float32), precision=lax.Precision.HIGHEST, preferred_element_type=jnp.float32)
    pivot_block = kernel_block(second_points, second_points) - jnp.dot(earlier_rows.astype(jnp.float32), earlier_rows.T.astype(jnp.float32), precision=lax.Precision.HIGHEST, preferred_element_type=jnp.float32)
    second_factor = new_columns(columns, pivot_block)
    residual_diag = 1.0 - jnp.sum(first_factor * first_factor, axis=1)
    residual_diag = residual_diag - jnp.sum(second_factor * second_factor, axis=1)
    return (jnp.concatenate([first_factor, second_factor], axis=1), residual_diag)
```

```python
import functools

import jax
import jax.numpy as jnp
from jax import lax
from jax.experimental import pallas as pl
from jax.experimental.pallas import tpu as pltpu
from jax.sharding import PartitionSpec as P

HIGHEST = lax.Precision.HIGHEST
MESH = pl.DeviceIdType.MESH
SUB = 8
TILE = 1024


def gather_kernel(count, feat_size, pivots, frames, points, held, mine, came, full, load_sem, s1, r1, s2, r2):
    me = lax.axis_index("dp") * feat_size + lax.axis_index("feat")
    row_count = frames.shape[0]
    start = me * row_count
    share = mine.shape[1]
    block = pivots.shape[1]

    load = pltpu.make_async_copy(frames, held, load_sem)
    load.start()

    def device(index):
        return {"dp": index // feat_size, "feat": index % feat_size}

    barrier = pltpu.get_barrier_semaphore()

    def greet(step, carry):
        other = lax.rem(me + step, count)
        pl.semaphore_signal(barrier, inc=1, device_id=device(other), device_id_type=MESH)
        return carry

    lax.fori_loop(1, count, greet, 0)
    load.wait()

    def pick(owner, carry):
        for k in range(share):
            slot = owner * share + k
            local = pivots[slot // block, slot % block] - start
            is_mine = (local >= 0) & (local < row_count)
            row = held[pl.ds(jnp.clip(local, 0, row_count - 1), 1), :]
            mine[owner, pl.ds(k, 1), :] = row * jnp.where(is_mine, 1.0, 0.0)
        return carry

    lax.fori_loop(0, count, pick, 0)
    pl.semaphore_wait(barrier, count - 1)

    def collect(step):
        other = lax.rem(me + step, count)
        return pltpu.make_async_remote_copy(
            src_ref=mine.at[other],
            dst_ref=came.at[step],
            send_sem=s1.at[step],
            recv_sem=r1.at[step],
            device_id=device(other),
            device_id_type=MESH,
        )

    def spread(step):
        other = lax.rem(me + step, count)
        return pltpu.make_async_remote_copy(
            src_ref=full.at[me],
            dst_ref=full.at[me],
            send_sem=s2.at[step],
            recv_sem=r2.at[step],
            device_id=device(other),
            device_id_type=MESH,
        )

    def spread_arrival(step):
        source = lax.rem(me + count - step, count)
        return pltpu.make_async_remote_copy(
            src_ref=full.at[source],
            dst_ref=full.at[source],
            send_sem=s2.at[step],
            recv_sem=r2.at[step],
            device_id=device(source),
            device_id_type=MESH,
        )

    def run(action):
        def body(step, carry):
            action(step)
            return carry

        lax.fori_loop(1, count, body, 0)

    run(lambda step: collect(step).start())

    def add(step, total):
        collect(step).wait_recv()
        return total + came[step]

    full[me] = lax.fori_loop(1, count, add, mine[me])
    run(lambda step: spread(step).start())
    run(lambda step: spread_arrival(step).wait_recv())
    run(lambda step: collect(step).wait_send())
    run(lambda step: spread(step).wait_send())
    points[...] = full[...]


def gather_points(mesh, frames, pivots):
    count = mesh.shape["dp"] * mesh.shape["feat"]
    blocks, block = pivots.shape
    slots = blocks * block
    share = slots // count
    feat = frames.shape[1]
    table = (count, share, feat)
    sems = pltpu.SemaphoreType.DMA((count,))
    points = pl.pallas_call(
        functools.partial(gather_kernel, count, mesh.shape["feat"]),
        out_shape=jax.ShapeDtypeStruct(table, jnp.float32),
        in_specs=[pl.BlockSpec(memory_space=pltpu.SMEM), pl.BlockSpec(memory_space=pl.ANY)],
        out_specs=pl.BlockSpec(memory_space=pltpu.VMEM),
        scratch_shapes=[
            pltpu.VMEM(frames.shape, jnp.float32),
            pltpu.VMEM(table, jnp.float32),
            pltpu.VMEM(table, jnp.float32),
            pltpu.VMEM(table, jnp.float32),
            pltpu.SemaphoreType.DMA(()),
            sems,
            sems,
            sems,
            sems,
        ],
        compiler_params=pltpu.CompilerParams(
            collective_id=0, has_side_effects=True, vmem_limit_bytes=16 * 1024 * 1024
        ),
    )(pivots, frames)
    return points.reshape(slots, feat)


def dot(left, right, dims=((1,), (0,)), precision=None):
    return lax.dot_general(
        left, right, (dims, ((), ())), precision=precision, preferred_element_type=jnp.float32
    )


def halves(value):
    high = value.astype(jnp.bfloat16)
    return high, (value - high.astype(jnp.float32)).astype(jnp.bfloat16)


def inverse_factor(matrix):
    size = matrix.shape[0]
    rows = [matrix[i * SUB : (i + 1) * SUB, :] for i in range(size // SUB)]
    sub = lax.broadcasted_iota(jnp.int32, (SUB, size), 0)
    lane = lax.broadcasted_iota(jnp.int32, (SUB, size), 1)

    def column(value, index):
        return jnp.broadcast_to(value[:, index : index + 1], (SUB, size))

    def row(value, index):
        return jnp.broadcast_to(value[index : index + 1, :], (SUB, size))

    out = []
    for k in range(size // SUB):
        base = k * SUB
        in_block = (lane >= base) & (lane < base + SUB)
        cols = [column(rows[k], base + j) for j in range(SUB)]
        work = jnp.where(in_block, jnp.where(lane - base == sub, 1.0, 0.0), rows[k])
        done = jnp.zeros((SUB, size), jnp.float32)
        for j in range(SUB):
            pivot = row(cols[j], j)
            inverse = 1.0 / pivot
            pivot_row = row(work, j)
            done = jnp.where(sub == j, pivot_row * lax.rsqrt(pivot), done)
            scaled = cols[j] * inverse
            work = jnp.where(sub == j, pivot_row * inverse, work - scaled * pivot_row)
            for m in range(j + 1, SUB):
                pivot_col = row(cols[m], j)
                cols[m] = jnp.where(sub == j, pivot_col * inverse, cols[m] - scaled * pivot_col)
        out.append(jnp.where(lane <= base + sub, done, 0.0))
        reduced = [row(work, j) for j in range(SUB)]
        for i in range(k + 1, size // SUB):
            update = [column(rows[i], base + j) * reduced[j] for j in range(SUB)]
            while len(update) > 1:
                update = [a + b for a, b in zip(update[::2], update[1::2])]
            rows[i] = jnp.where(in_block, 0.0, rows[i]) - update[0]
    return jnp.concatenate(out, axis=0)


def factor_kernel(points, frames, factor, residual, pts_hi, pts_lo, norms, wt_hi, wt_lo):
    feat = points.shape[1]
    block = points.shape[0] // 2
    scale = -0.5 / feat

    @pl.when(pl.program_id(0) == 0)
    def _():
        pts = points[...]
        squares = pts * pts
        ones = jnp.ones((SUB, feat), jnp.float32)
        row_norms = dot(ones, squares, ((1,), (1,)), HIGHEST)
        norms[...] = row_norms
        products = dot(pts, pts, ((1,), (1,)), HIGHEST)
        gram = jnp.exp(
            (jnp.sum(squares, axis=1, keepdims=True) + row_norms[:1] - 2.0 * products) * scale
        )
        first = inverse_factor(gram[:block, :block])
        earlier = dot(gram[block:, :block], first, ((1,), (1,)), HIGHEST)
        second = inverse_factor(
            gram[block:, block:] - dot(earlier, earlier, ((1,), (1,)), HIGHEST)
        )
        mixed = -dot(second, dot(earlier, first, precision=HIGHEST), precision=HIGHEST)
        whole = jnp.concatenate(
            [
                jnp.concatenate([first, jnp.zeros_like(first)], axis=1),
                jnp.concatenate([mixed, second], axis=1),
            ],
            axis=0,
        ).T
        high, low = halves(whole)
        wt_hi[...] = high
        wt_lo[...] = low
        high, low = halves(pts.T)
        pts_hi[...] = high
        pts_lo[...] = low

    tile = frames[...]
    tile_norms = jnp.sum(tile * tile, axis=1, keepdims=True)
    high, low = halves(tile)
    both = jnp.concatenate([high, low], axis=1)
    products = dot(both, jnp.concatenate([pts_hi[...]] * 2, axis=0)) + dot(high, pts_lo[...])
    kern = jnp.exp((tile_norms + norms[:1] - 2.0 * products) * scale)
    high, low = halves(kern)
    result = dot(high, wt_hi[...]) + dot(low, wt_hi[...]) + dot(high, wt_lo[...])
    factor[...] = result
    high, low = halves(result * result)
    ones = jnp.ones((SUB, result.shape[1]), jnp.bfloat16)
    sums = dot(ones, high, ((1,), (1,))) + dot(ones, low, ((1,), (1,)))
    residual[0] = 1.0 - sums[:1]


def shards(mesh, frames, pivots):
    points = gather_points(mesh, frames, pivots)
    row_count, feat = frames.shape
    slots = points.shape[0]
    tiles = row_count // TILE
    factor, residual = pl.pallas_call(
        factor_kernel,
        grid=(tiles,),
        out_shape=(
            jax.ShapeDtypeStruct((row_count, slots), jnp.float32),
            jax.ShapeDtypeStruct((tiles, 1, TILE), jnp.float32),
        ),
        in_specs=[
            pl.BlockSpec((slots, feat), lambda i: (0, 0)),
            pl.BlockSpec((TILE, feat), lambda i: (i, 0)),
        ],
        out_specs=(
            pl.BlockSpec((TILE, slots), lambda i: (i, 0)),
            pl.BlockSpec((1, 1, TILE), lambda i: (i, 0, 0)),
        ),
        scratch_shapes=[
            pltpu.VMEM((feat, slots), jnp.bfloat16),
            pltpu.VMEM((feat, slots), jnp.bfloat16),
            pltpu.VMEM((SUB, slots), jnp.float32),
            pltpu.VMEM((slots, slots), jnp.bfloat16),
            pltpu.VMEM((slots, slots), jnp.bfloat16),
        ],
        compiler_params=pltpu.CompilerParams(vmem_limit_bytes=40 * 1024 * 1024),
    )(points, frames)
    return factor, residual.reshape(row_count)


def solution(mesh):
    placed = (P(("groups", "dp", "feat"), None), P("groups", None))
    return jax.shard_map(
        functools.partial(shards, mesh),
        mesh=mesh,
        in_specs=placed,
        out_specs=(P(("groups", "dp", "feat"), None), P(("groups", "dp", "feat"))),
        check_vma=False,
    )
```

```python
import functools
import math

import jax
import jax.numpy as jnp
from jax import lax
from jax.experimental import pallas as pl
from jax.experimental.pallas import tpu as pltpu
from jax.sharding import PartitionSpec as P

HIGHEST = lax.Precision.HIGHEST
MESH = pl.DeviceIdType.MESH
SUB = 8
TILE = 1024


def gather_kernel(count, feat_size, pivots, frames, points, held, mine, came, full, load_sem, s1, r1, s2, r2):
    me = lax.axis_index("dp") * feat_size + lax.axis_index("feat")
    row_count = frames.shape[0]
    start = me * row_count
    share = mine.shape[1]
    block = pivots.shape[1]

    load = pltpu.make_async_copy(frames, held, load_sem)
    load.start()

    def device(index):
        return {"dp": index // feat_size, "feat": index % feat_size}

    barrier = pltpu.get_barrier_semaphore()

    def greet(step, carry):
        other = lax.rem(me + step, count)
        pl.semaphore_signal(barrier, inc=1, device_id=device(other), device_id_type=MESH)
        return carry

    lax.fori_loop(1, count, greet, 0)
    load.wait()

    def pick(owner, carry):
        for k in range(share):
            slot = owner * share + k
            local = pivots[slot // block, slot % block] - start
            is_mine = (local >= 0) & (local < row_count)
            row = held[pl.ds(jnp.clip(local, 0, row_count - 1), 1), :]
            mine[owner, pl.ds(k, 1), :] = row * jnp.where(is_mine, 1.0, 0.0)
        return carry

    lax.fori_loop(0, count, pick, 0)
    pl.semaphore_wait(barrier, count - 1)

    def collect(step):
        other = lax.rem(me + step, count)
        return pltpu.make_async_remote_copy(
            src_ref=mine.at[other],
            dst_ref=came.at[step],
            send_sem=s1.at[step],
            recv_sem=r1.at[step],
            device_id=device(other),
            device_id_type=MESH,
        )

    def spread(step):
        other = lax.rem(me + step, count)
        return pltpu.make_async_remote_copy(
            src_ref=full.at[me],
            dst_ref=full.at[me],
            send_sem=s2.at[step],
            recv_sem=r2.at[step],
            device_id=device(other),
            device_id_type=MESH,
        )

    def spread_arrival(step):
        source = lax.rem(me + count - step, count)
        return pltpu.make_async_remote_copy(
            src_ref=full.at[source],
            dst_ref=full.at[source],
            send_sem=s2.at[step],
            recv_sem=r2.at[step],
            device_id=device(source),
            device_id_type=MESH,
        )

    def run(action):
        def body(step, carry):
            action(step)
            return carry

        lax.fori_loop(1, count, body, 0)

    run(lambda step: collect(step).start())

    def add(step, total):
        collect(step).wait_recv()
        return total + came[step]

    full[me] = lax.fori_loop(1, count, add, mine[me])
    run(lambda step: spread(step).start())
    run(lambda step: spread_arrival(step).wait_recv())
    run(lambda step: collect(step).wait_send())
    run(lambda step: spread(step).wait_send())
    points[...] = full[...]


def gather_points(mesh, frames, pivots):
    count = mesh.shape["dp"] * mesh.shape["feat"]
    blocks, block = pivots.shape
    slots = blocks * block
    share = slots // count
    feat = frames.shape[1]
    table = (count, share, feat)
    sems = pltpu.SemaphoreType.DMA((count,))
    points = pl.pallas_call(
        functools.partial(gather_kernel, count, mesh.shape["feat"]),
        out_shape=jax.ShapeDtypeStruct(table, jnp.float32),
        in_specs=[pl.BlockSpec(memory_space=pltpu.SMEM), pl.BlockSpec(memory_space=pl.ANY)],
        out_specs=pl.BlockSpec(memory_space=pltpu.VMEM),
        scratch_shapes=[
            pltpu.VMEM(frames.shape, jnp.float32),
            pltpu.VMEM(table, jnp.float32),
            pltpu.VMEM(table, jnp.float32),
            pltpu.VMEM(table, jnp.float32),
            pltpu.SemaphoreType.DMA(()),
            sems,
            sems,
            sems,
            sems,
        ],
        compiler_params=pltpu.CompilerParams(
            collective_id=0, has_side_effects=True, vmem_limit_bytes=60 * 1024 * 1024
        ),
    )(pivots, frames)
    return points.reshape(slots, feat)


def dot(left, right, dims=((1,), (0,)), precision=None):
    return lax.dot_general(
        left, right, (dims, ((), ())), precision=precision, preferred_element_type=jnp.float32
    )


def halves(value):
    high = value.astype(jnp.bfloat16)
    return high, (value - high.astype(jnp.float32)).astype(jnp.bfloat16)


def inverse_factor(matrix):
    size = matrix.shape[0]
    rows = [matrix[i * SUB : (i + 1) * SUB, :] for i in range(size // SUB)]
    sub = lax.broadcasted_iota(jnp.int32, (SUB, size), 0)
    lane = lax.broadcasted_iota(jnp.int32, (SUB, size), 1)

    def column(value, index):
        return jnp.broadcast_to(value[:, index : index + 1], (SUB, size))

    def row(value, index):
        return jnp.broadcast_to(value[index : index + 1, :], (SUB, size))

    out = []
    for k in range(size // SUB):
        base = k * SUB
        in_block = (lane >= base) & (lane < base + SUB)
        cols = [column(rows[k], base + j) for j in range(SUB)]
        work = jnp.where(in_block, jnp.where(lane - base == sub, 1.0, 0.0), rows[k])
        done = jnp.zeros((SUB, size), jnp.float32)
        for j in range(SUB):
            pivot = row(cols[j], j)
            inverse = 1.0 / pivot
            pivot_row = row(work, j)
            done = jnp.where(sub == j, pivot_row * lax.rsqrt(pivot), done)
            scaled = cols[j] * inverse
            work = jnp.where(sub == j, pivot_row * inverse, work - scaled * pivot_row)
            for m in range(j + 1, SUB):
                pivot_col = row(cols[m], j)
                cols[m] = jnp.where(sub == j, pivot_col * inverse, cols[m] - scaled * pivot_col)
        out.append(jnp.where(lane <= base + sub, done, 0.0))
        reduced = [row(work, j) for j in range(SUB)]
        for i in range(k + 1, size // SUB):
            update = [column(rows[i], base + j) * reduced[j] for j in range(SUB)]
            while len(update) > 1:
                update = [a + b for a, b in zip(update[::2], update[1::2])]
            rows[i] = jnp.where(in_block, 0.0, rows[i]) - update[0]
    return jnp.concatenate(out, axis=0)


def factor_kernel(points, frames, factor, residual, pts, wt):
    feat = points.shape[1]
    slots = points.shape[0]
    block = slots // 2
    fold = -0.5 / feat * math.log2(math.e)

    @pl.when(pl.program_id(0) == 0)
    def _():
        table = points[...]
        squares = table * table
        ones = jnp.ones((SUB, feat), jnp.float32)
        norms = fold * dot(ones, squares, ((1,), (1,)), HIGHEST)
        products = dot(table, table, ((1,), (1,)), HIGHEST)
        gram = jnp.exp2(
            (fold * jnp.sum(squares, axis=1, keepdims=True) + norms[:1]) - 2.0 * fold * products
        )
        first = inverse_factor(gram[:block, :block])
        earlier = dot(gram[block:, :block], first, ((1,), (1,)), HIGHEST)
        second = inverse_factor(
            gram[block:, block:] - dot(earlier, earlier, ((1,), (1,)), HIGHEST)
        )
        mixed = -dot(second, dot(earlier, first, precision=HIGHEST), precision=HIGHEST)
        whole = jnp.concatenate(
            [
                jnp.concatenate([first, jnp.zeros_like(first)], axis=1),
                jnp.concatenate([mixed, second], axis=1),
            ],
            axis=0,
        ).T
        high, low = halves(whole)
        wt[...] = jnp.concatenate([high, high, low], axis=0)
        high, low = halves((-2.0 * fold) * table.T)
        n_high, n_rest = halves(norms)
        rest = norms - n_high.astype(jnp.float32)
        n_low = (rest - n_rest.astype(jnp.float32)).astype(jnp.bfloat16)
        row = lax.broadcasted_iota(jnp.int32, (feat, slots), 0)
        extra = jnp.where(
            row == 0,
            n_high[:1].astype(jnp.float32),
            jnp.where(
                row == 1,
                n_rest[:1].astype(jnp.float32),
                jnp.where(row == 2, n_low[:1].astype(jnp.float32), 0.0),
            ),
        ).astype(jnp.bfloat16)
        pts[...] = jnp.concatenate([high, high, low, extra], axis=0)

    tile = frames[...]
    tile_norms = fold * jnp.sum(tile * tile, axis=1, keepdims=True)
    high, low = halves(tile)
    exponent = dot(
        jnp.concatenate([high, low, high, jnp.ones_like(high)], axis=1), pts[...]
    )
    high, low = halves(jnp.exp2(tile_norms + exponent))
    result = dot(jnp.concatenate([high, low, high], axis=1), wt[...])
    factor[...] = result
    squares = result[:, :block] * result[:, :block] + result[:, block:] * result[:, block:]
    residual[0] = 1.0 - jnp.sum(squares.T, axis=0, keepdims=True)


def shards(mesh, frames, pivots):
    points = gather_points(mesh, frames, pivots)
    row_count, feat = frames.shape
    slots = points.shape[0]
    tiles = row_count // TILE
    factor, residual = pl.pallas_call(
        factor_kernel,
        grid=(tiles,),
        out_shape=(
            jax.ShapeDtypeStruct((row_count, slots), jnp.float32),
            jax.ShapeDtypeStruct((tiles, 1, TILE), jnp.float32),
        ),
        in_specs=[
            pl.BlockSpec((slots, feat), lambda i: (0, 0)),
            pl.BlockSpec((TILE, feat), lambda i: (i, 0)),
        ],
        out_specs=(
            pl.BlockSpec((TILE, slots), lambda i: (i, 0)),
            pl.BlockSpec((1, 1, TILE), lambda i: (i, 0, 0)),
        ),
        scratch_shapes=[
            pltpu.VMEM((4 * feat, slots), jnp.bfloat16),
            pltpu.VMEM((3 * slots, slots), jnp.bfloat16),
        ],
        compiler_params=pltpu.CompilerParams(vmem_limit_bytes=60 * 1024 * 1024),
    )(points, frames)
    return factor, residual.reshape(row_count)


def solution(mesh):
    placed = (P(("groups", "dp", "feat"), None), P("groups", None))
    return jax.shard_map(
        functools.partial(shards, mesh),
        mesh=mesh,
        in_specs=placed,
        out_specs=(P(("groups", "dp", "feat"), None), P(("groups", "dp", "feat"))),
        check_vma=False,
    )
```

```python
import functools
import math

import jax
import jax.numpy as jnp
from jax import lax
from jax.experimental import pallas as pl
from jax.experimental.pallas import tpu as pltpu
from jax.sharding import PartitionSpec as P

HIGHEST = lax.Precision.HIGHEST
MESH = pl.DeviceIdType.MESH
SUB = 8


def gather_kernel(count, feat_size, pivots, frames, points, held, mine, came, full, load_sem, s1, r1, s2, r2):
    me = lax.axis_index("dp") * feat_size + lax.axis_index("feat")
    row_count = frames.shape[0]
    start = me * row_count
    share = mine.shape[1]
    block = pivots.shape[1]

    load = pltpu.make_async_copy(frames, held, load_sem)
    load.start()

    def device(index):
        return {"dp": index // feat_size, "feat": index % feat_size}

    barrier = pltpu.get_barrier_semaphore()

    def greet(step, carry):
        other = lax.rem(me + step, count)
        pl.semaphore_signal(barrier, inc=1, device_id=device(other), device_id_type=MESH)
        return carry

    lax.fori_loop(1, count, greet, 0)
    load.wait()

    def pick(owner, carry):
        for k in range(share):
            slot = owner * share + k
            local = pivots[slot // block, slot % block] - start
            is_mine = (local >= 0) & (local < row_count)
            row = held[pl.ds(jnp.clip(local, 0, row_count - 1), 1), :]
            mine[owner, pl.ds(k, 1), :] = row * jnp.where(is_mine, 1.0, 0.0)
        return carry

    lax.fori_loop(0, count, pick, 0)
    pl.semaphore_wait(barrier, count - 1)

    def collect(step):
        other = lax.rem(me + step, count)
        return pltpu.make_async_remote_copy(
            src_ref=mine.at[other],
            dst_ref=came.at[step],
            send_sem=s1.at[step],
            recv_sem=r1.at[step],
            device_id=device(other),
            device_id_type=MESH,
        )

    def spread(step):
        other = lax.rem(me + step, count)
        return pltpu.make_async_remote_copy(
            src_ref=full.at[me],
            dst_ref=full.at[me],
            send_sem=s2.at[step],
            recv_sem=r2.at[step],
            device_id=device(other),
            device_id_type=MESH,
        )

    def spread_arrival(step):
        source = lax.rem(me + count - step, count)
        return pltpu.make_async_remote_copy(
            src_ref=full.at[source],
            dst_ref=full.at[source],
            send_sem=s2.at[step],
            recv_sem=r2.at[step],
            device_id=device(source),
            device_id_type=MESH,
        )

    def run(action):
        def body(step, carry):
            action(step)
            return carry

        lax.fori_loop(1, count, body, 0)

    run(lambda step: collect(step).start())

    def add(step, total):
        collect(step).wait_recv()
        return total + came[step]

    full[me] = lax.fori_loop(1, count, add, mine[me])
    run(lambda step: spread(step).start())
    run(lambda step: spread_arrival(step).wait_recv())
    run(lambda step: collect(step).wait_send())
    run(lambda step: spread(step).wait_send())
    points[...] = full[...]


def gather_points(mesh, frames, pivots):
    count = mesh.shape["dp"] * mesh.shape["feat"]
    blocks, block = pivots.shape
    slots = blocks * block
    share = slots // count
    feat = frames.shape[1]
    table = (count, share, feat)
    sems = pltpu.SemaphoreType.DMA((count,))
    points = pl.pallas_call(
        functools.partial(gather_kernel, count, mesh.shape["feat"]),
        out_shape=jax.ShapeDtypeStruct(table, jnp.float32),
        in_specs=[pl.BlockSpec(memory_space=pltpu.SMEM), pl.BlockSpec(memory_space=pl.ANY)],
        out_specs=pl.BlockSpec(memory_space=pltpu.VMEM),
        scratch_shapes=[
            pltpu.VMEM(frames.shape, jnp.float32),
            pltpu.VMEM(table, jnp.float32),
            pltpu.VMEM(table, jnp.float32),
            pltpu.VMEM(table, jnp.float32),
            pltpu.SemaphoreType.DMA(()),
            sems,
            sems,
            sems,
            sems,
        ],
        compiler_params=pltpu.CompilerParams(
            collective_id=0, has_side_effects=True, vmem_limit_bytes=60 * 1024 * 1024
        ),
    )(pivots, frames)
    return points.reshape(slots, feat)


def dot(left, right, dims=((1,), (0,)), precision=None):
    return lax.dot_general(
        left, right, (dims, ((), ())), precision=precision, preferred_element_type=jnp.float32
    )


def halves(value):
    high = value.astype(jnp.bfloat16)
    return high, (value - high.astype(jnp.float32)).astype(jnp.bfloat16)


def inverse_factor(matrix, beside):
    size = matrix.shape[0]
    rows = [matrix[i * SUB : (i + 1) * SUB, :] for i in range(size // SUB)]
    sub = lax.broadcasted_iota(jnp.int32, (SUB, size), 0)
    lane = lax.broadcasted_iota(jnp.int32, (SUB, size), 1)

    def column(value, index):
        return jnp.broadcast_to(value[:, index : index + 1], (SUB, size))

    def row(value, index):
        return jnp.broadcast_to(value[index : index + 1, :], (SUB, size))

    out = []
    for k in range(size // SUB):
        base = k * SUB
        in_block = (lane >= base) & (lane < base + SUB)
        cols = [column(rows[k], base + j) for j in range(SUB)]
        work = jnp.where(in_block, jnp.where(lane - base == sub, 1.0, 0.0), rows[k])
        done = jnp.zeros((SUB, size), jnp.float32)
        for j in range(SUB):
            pivot = row(cols[j], j)
            inverse = 1.0 / pivot
            pivot_row = row(work, j)
            done = jnp.where(sub == j, pivot_row * lax.rsqrt(pivot), done)
            scaled = cols[j] * inverse
            work = jnp.where(sub == j, pivot_row * inverse, work - scaled * pivot_row)
            for m in range(j + 1, SUB):
                pivot_col = row(cols[m], j)
                cols[m] = jnp.where(sub == j, pivot_col * inverse, cols[m] - scaled * pivot_col)
        beside(k)
        out.append(jnp.where(lane <= base + sub, done, 0.0))
        reduced = [row(work, j) for j in range(SUB)]
        for i in range(k + 1, size // SUB):
            update = [column(rows[i], base + j) * reduced[j] for j in range(SUB)]
            while len(update) > 1:
                update = [a + b for a, b in zip(update[::2], update[1::2])]
            rows[i] = jnp.where(in_block, 0.0, rows[i]) - update[0]
    return jnp.concatenate(out, axis=0)


def factor_kernel(
    points, frames, factor, residual, held, pts, k_hi, k_lo, out1, out2, w_first, w_hi, w_lo,
    load_sem, sem1, sem2,
):
    slots, feat = points.shape
    block = slots // 2
    row_count = frames.shape[0]
    chunks = block // SUB
    chunk = row_count // chunks
    half = row_count // 2
    group = chunks // sem1.shape[0]
    fold = -0.5 / feat * math.log2(math.e)

    def load(part):
        rows = pl.ds(part * half, half)
        return pltpu.make_async_copy(frames.at[rows, :], held.at[rows, :], load_sem.at[part])

    def store1(part):
        rows = pl.ds(part * group * chunk, group * chunk)
        return pltpu.make_async_copy(
            out1.at[rows, :], factor.at[rows, pl.ds(0, block)], sem1.at[part]
        )

    def store2(part):
        rows = pl.ds(part * chunk, chunk)
        return pltpu.make_async_copy(
            out2.at[rows, :], factor.at[rows, pl.ds(block, block)], sem2.at[part]
        )

    load(0).start()
    load(1).start()

    table = points[...]
    squares = table * table
    ones = jnp.ones((SUB, feat), jnp.float32)
    norms = fold * dot(ones, squares, ((1,), (1,)), HIGHEST)
    products = dot(table, table, ((1,), (1,)), HIGHEST)
    gram = jnp.exp2(
        (fold * jnp.sum(squares, axis=1, keepdims=True) + norms[:1]) - 2.0 * fold * products
    )
    high, low = halves((-2.0 * fold) * table.T)
    n_high, n_rest = halves(norms)
    rest = norms - n_high.astype(jnp.float32)
    n_low = (rest - n_rest.astype(jnp.float32)).astype(jnp.bfloat16)
    row = lax.broadcasted_iota(jnp.int32, (feat, slots), 0)
    extra = jnp.where(
        row == 0,
        n_high[:1].astype(jnp.float32),
        jnp.where(
            row == 1,
            n_rest[:1].astype(jnp.float32),
            jnp.where(row == 2, n_low[:1].astype(jnp.float32), 0.0),
        ),
    ).astype(jnp.bfloat16)
    pts[...] = jnp.concatenate([high, high, low, extra], axis=0)
    load(0).wait()

    def kern_chunk(k):
        if k == chunks // 2:
            load(1).wait()
        rows = pl.ds(k * chunk, chunk)
        tile = held[rows, :]
        tile_norms = fold * jnp.sum(tile * tile, axis=1, keepdims=True)
        high, low = halves(tile)
        exponent = dot(
            jnp.concatenate([high, low, high, jnp.ones_like(high)], axis=1), pts[...]
        )
        high, low = halves(jnp.exp2(tile_norms + exponent))
        k_hi[rows, :] = high
        k_lo[rows, :] = low

    first = inverse_factor(gram[:block, :block], kern_chunk)
    earlier = dot(gram[block:, :block], first, ((1,), (1,)), HIGHEST)
    schur = gram[block:, block:] - dot(earlier, earlier, ((1,), (1,)), HIGHEST)
    high, low = halves(first.T)
    w_first[...] = jnp.concatenate(
        [
            jnp.concatenate([high, low], axis=1),
            jnp.concatenate([high, jnp.zeros_like(high)], axis=1),
        ],
        axis=0,
    )
    carried = dot(earlier, first, precision=HIGHEST)

    def first_chunk(k):
        rows = pl.ds(k * chunk, chunk)
        both = jnp.concatenate([k_hi[rows, :block], k_lo[rows, :block]], axis=1)
        result = dot(both, w_first[...])
        out1[rows, :] = result[:, :block] + result[:, block:]
        if k % group == group - 1:
            store1(k // group).start()

    second = inverse_factor(schur, first_chunk)
    mixed = -dot(second, carried, precision=HIGHEST)
    high, low = halves(jnp.concatenate([mixed, second], axis=1).T)
    w_hi[...] = jnp.concatenate([high, low], axis=1)
    w_lo[...] = high

    def second_chunk(k, carry):
        rows = pl.ds(pl.multiple_of(k * chunk, chunk), chunk)
        wide = dot(k_hi[rows, :], w_hi[...])
        result = wide[:, :block] + wide[:, block:] + dot(k_lo[rows, :], w_lo[...])
        out2[rows, :] = result
        store2(k).start()
        before = out1[rows, :]
        squares = before * before + result * result
        residual[k] = 1.0 - jnp.sum(squares.T, axis=0, keepdims=True)
        return carry

    lax.fori_loop(0, chunks, second_chunk, 0)
    for k in range(chunks // group):
        store1(k).wait()

    def finish(k, carry):
        store2(k).wait()
        return carry

    lax.fori_loop(0, chunks, finish, 0)


def shards(mesh, frames, pivots):
    points = gather_points(mesh, frames, pivots)
    row_count, feat = frames.shape
    slots = points.shape[0]
    block = slots // 2
    chunks = block // SUB
    vmem = pl.BlockSpec(memory_space=pltpu.VMEM)
    anywhere = pl.BlockSpec(memory_space=pl.ANY)
    factor, residual = pl.pallas_call(
        factor_kernel,
        out_shape=(
            jax.ShapeDtypeStruct((row_count, slots), jnp.float32),
            jax.ShapeDtypeStruct((chunks, 1, row_count // chunks), jnp.float32),
        ),
        in_specs=[vmem, anywhere],
        out_specs=(anywhere, vmem),
        scratch_shapes=[
            pltpu.VMEM((row_count, feat), jnp.float32),
            pltpu.VMEM((4 * feat, slots), jnp.bfloat16),
            pltpu.VMEM((row_count, slots), jnp.bfloat16),
            pltpu.VMEM((row_count, slots), jnp.bfloat16),
            pltpu.VMEM((row_count, block), jnp.float32),
            pltpu.VMEM((row_count, block), jnp.float32),
            pltpu.VMEM((slots, slots), jnp.bfloat16),
            pltpu.VMEM((slots, slots), jnp.bfloat16),
            pltpu.VMEM((slots, block), jnp.bfloat16),
            pltpu.SemaphoreType.DMA((2,)),
            pltpu.SemaphoreType.DMA((4,)),
            pltpu.SemaphoreType.DMA((chunks,)),
        ],
        compiler_params=pltpu.CompilerParams(vmem_limit_bytes=60 * 1024 * 1024),
    )(points, frames)
    return factor, residual.reshape(row_count)


def solution(mesh):
    placed = (P(("groups", "dp", "feat"), None), P("groups", None))
    return jax.shard_map(
        functools.partial(shards, mesh),
        mesh=mesh,
        in_specs=placed,
        out_specs=(P(("groups", "dp", "feat"), None), P(("groups", "dp", "feat"))),
        check_vma=False,
    )
```

```python
import functools
import math

import jax
import jax.numpy as jnp
from jax import lax
from jax.experimental import pallas as pl
from jax.experimental.pallas import tpu as pltpu
from jax.sharding import PartitionSpec as P

HIGHEST = lax.Precision.HIGHEST
MESH = pl.DeviceIdType.MESH
SUB = 8


def gather_kernel(count, feat_size, pivots, frames, points, held, mine, came, full, load_sem, s1, r1, s2, r2):
    me = lax.axis_index("dp") * feat_size + lax.axis_index("feat")
    row_count = frames.shape[0]
    start = me * row_count
    share = mine.shape[1]
    block = pivots.shape[1]

    parts = load_sem.shape[0]
    loads = []
    for part in range(parts):
        rows = pl.ds(part * (row_count // parts), row_count // parts)
        loads.append(
            pltpu.make_async_copy(frames.at[rows, :], held.at[rows, :], load_sem.at[part])
        )
    for load in loads:
        load.start()

    def device(index):
        return {"dp": index // feat_size, "feat": index % feat_size}

    barrier = pltpu.get_barrier_semaphore()

    def greet(step, carry):
        other = lax.rem(me + step, count)
        pl.semaphore_signal(barrier, inc=1, device_id=device(other), device_id_type=MESH)
        return carry

    lax.fori_loop(1, count, greet, 0)
    for load in loads:
        load.wait()

    def pick(owner):
        for k in range(share):
            slot = owner * share + k
            local = pivots[slot // block, slot % block] - start
            is_mine = (local >= 0) & (local < row_count)
            row = held[pl.ds(jnp.clip(local, 0, row_count - 1), 1), :]
            mine[owner, pl.ds(k, 1), :] = row * jnp.where(is_mine, 1.0, 0.0)

    pl.semaphore_wait(barrier, count - 1)

    def collect(step):
        other = lax.rem(me + step, count)
        return pltpu.make_async_remote_copy(
            src_ref=mine.at[other],
            dst_ref=came.at[step],
            send_sem=s1.at[step],
            recv_sem=r1.at[step],
            device_id=device(other),
            device_id_type=MESH,
        )

    def spread(step):
        other = lax.rem(me + step, count)
        return pltpu.make_async_remote_copy(
            src_ref=full.at[me],
            dst_ref=full.at[me],
            send_sem=s2.at[step],
            recv_sem=r2.at[step],
            device_id=device(other),
            device_id_type=MESH,
        )

    def spread_arrival(step):
        source = lax.rem(me + count - step, count)
        return pltpu.make_async_remote_copy(
            src_ref=full.at[source],
            dst_ref=full.at[source],
            send_sem=s2.at[step],
            recv_sem=r2.at[step],
            device_id=device(source),
            device_id_type=MESH,
        )

    def run(action):
        def body(step, carry):
            action(step)
            return carry

        lax.fori_loop(1, count, body, 0)

    def send(step):
        pick(lax.rem(me + step, count))
        collect(step).start()

    run(send)
    pick(me)

    def add(step, total):
        collect(step).wait_recv()
        return total + came[step]

    full[me] = lax.fori_loop(1, count, add, mine[me])
    run(lambda step: spread(step).start())
    run(lambda step: spread_arrival(step).wait_recv())
    run(lambda step: collect(step).wait_send())
    run(lambda step: spread(step).wait_send())
    points[...] = full[...]


def gather_points(mesh, frames, pivots):
    count = mesh.shape["dp"] * mesh.shape["feat"]
    blocks, block = pivots.shape
    slots = blocks * block
    share = slots // count
    feat = frames.shape[1]
    table = (count, share, feat)
    sems = pltpu.SemaphoreType.DMA((count,))
    points = pl.pallas_call(
        functools.partial(gather_kernel, count, mesh.shape["feat"]),
        out_shape=jax.ShapeDtypeStruct(table, jnp.float32),
        in_specs=[pl.BlockSpec(memory_space=pltpu.SMEM), pl.BlockSpec(memory_space=pl.ANY)],
        out_specs=pl.BlockSpec(memory_space=pltpu.VMEM),
        scratch_shapes=[
            pltpu.VMEM(frames.shape, jnp.float32),
            pltpu.VMEM(table, jnp.float32),
            pltpu.VMEM(table, jnp.float32),
            pltpu.VMEM(table, jnp.float32),
            pltpu.SemaphoreType.DMA((8,)),
            sems,
            sems,
            sems,
            sems,
        ],
        compiler_params=pltpu.CompilerParams(
            collective_id=0, has_side_effects=True, vmem_limit_bytes=60 * 1024 * 1024
        ),
    )(pivots, frames)
    return points.reshape(slots, feat)


def dot(left, right, dims=((1,), (0,)), precision=None):
    return lax.dot_general(
        left, right, (dims, ((), ())), precision=precision, preferred_element_type=jnp.float32
    )


def halves(value):
    high = value.astype(jnp.bfloat16)
    return high, (value - high.astype(jnp.float32)).astype(jnp.bfloat16)


def inverse_factor(matrix, beside):
    size = matrix.shape[0]
    rows = [matrix[i * SUB : (i + 1) * SUB, :] for i in range(size // SUB)]
    sub = lax.broadcasted_iota(jnp.int32, (SUB, size), 0)
    lane = lax.broadcasted_iota(jnp.int32, (SUB, size), 1)

    def column(value, index):
        return jnp.broadcast_to(value[:, index : index + 1], (SUB, size))

    def row(value, index):
        return jnp.broadcast_to(value[index : index + 1, :], (SUB, size))

    out = []
    for k in range(size // SUB):
        base = k * SUB
        in_block = (lane >= base) & (lane < base + SUB)
        cols = [column(rows[k], base + j) for j in range(SUB)]
        work = jnp.where(in_block, jnp.where(lane - base == sub, 1.0, 0.0), rows[k])
        done = jnp.zeros((SUB, size), jnp.float32)
        for j in range(SUB):
            pivot = row(cols[j], j)
            inverse = 1.0 / pivot
            pivot_row = row(work, j)
            done = jnp.where(sub == j, pivot_row * lax.rsqrt(pivot), done)
            weight = jnp.where(sub == j, pivot - 1.0, cols[j])
            work = work - (weight * pivot_row) * inverse
            for m in range(j + 1, SUB):
                pivot_col = row(cols[m], j)
                cols[m] = cols[m] - (weight * pivot_col) * inverse
        beside(k)
        out.append(jnp.where(lane <= base + sub, done, 0.0))
        reduced = [row(work, j) for j in range(SUB)]
        for i in range(k + 1, size // SUB):
            update = [column(rows[i], base + j) * reduced[j] for j in range(SUB)]
            while len(update) > 1:
                update = [a + b for a, b in zip(update[::2], update[1::2])]
            rows[i] = jnp.where(in_block, 0.0, rows[i]) - update[0]
    return jnp.concatenate(out, axis=0)


def factor_kernel(
    points, frames, factor, residual, held, pts, k_hi, k_lo, out1, out2, w_first, w_hi, w_lo,
    load_sem, sem1, sem2,
):
    slots, feat = points.shape
    block = slots // 2
    row_count = frames.shape[0]
    chunks = block // SUB
    chunk = row_count // chunks
    half = row_count // 2
    group = chunks // sem1.shape[0]
    fold = -0.5 / feat * math.log2(math.e)

    def load(part):
        rows = pl.ds(part * half, half)
        return pltpu.make_async_copy(frames.at[rows, :], held.at[rows, :], load_sem.at[part])

    def store1(part):
        rows = pl.ds(part * group * chunk, group * chunk)
        return pltpu.make_async_copy(
            out1.at[rows, :], factor.at[rows, pl.ds(0, block)], sem1.at[part]
        )

    def store2(part):
        rows = pl.ds(part * chunk, chunk)
        return pltpu.make_async_copy(
            out2.at[rows, :], factor.at[rows, pl.ds(block, block)], sem2.at[part]
        )

    load(0).start()
    load(1).start()

    table = points[...]
    squares = table * table
    ones = jnp.ones((SUB, feat), jnp.float32)
    norms = fold * dot(ones, squares, ((1,), (1,)), HIGHEST)
    products = dot(table, table, ((1,), (1,)), HIGHEST)
    gram = jnp.exp2(
        (fold * jnp.sum(squares, axis=1, keepdims=True) + norms[:1]) - 2.0 * fold * products
    )
    high, low = halves((-2.0 * fold) * table.T)
    n_high, n_rest = halves(norms)
    rest = norms - n_high.astype(jnp.float32)
    n_low = (rest - n_rest.astype(jnp.float32)).astype(jnp.bfloat16)
    row = lax.broadcasted_iota(jnp.int32, (feat, slots), 0)
    extra = jnp.where(
        row == 0,
        n_high[:1].astype(jnp.float32),
        jnp.where(
            row == 1,
            n_rest[:1].astype(jnp.float32),
            jnp.where(row == 2, n_low[:1].astype(jnp.float32), 0.0),
        ),
    ).astype(jnp.bfloat16)
    pts[...] = jnp.concatenate([high, high, low, extra], axis=0)
    load(0).wait()

    def kern_chunk(k):
        if k == chunks // 2:
            load(1).wait()
        rows = pl.ds(k * chunk, chunk)
        tile = held[rows, :]
        tile_norms = fold * jnp.sum(tile * tile, axis=1, keepdims=True)
        high, low = halves(tile)
        exponent = dot(
            jnp.concatenate([high, low, high, jnp.ones_like(high)], axis=1), pts[...]
        )
        high, low = halves(jnp.exp2(tile_norms + exponent))
        k_hi[rows, :] = high
        k_lo[rows, :] = low

    first = inverse_factor(gram[:block, :block], kern_chunk)
    earlier = dot(gram[block:, :block], first, ((1,), (1,)), HIGHEST)
    schur = gram[block:, block:] - dot(earlier, earlier, ((1,), (1,)), HIGHEST)
    high, low = halves(first.T)
    w_first[...] = jnp.concatenate(
        [
            jnp.concatenate([high, low], axis=1),
            jnp.concatenate([high, jnp.zeros_like(high)], axis=1),
        ],
        axis=0,
    )
    carried = dot(earlier, first, precision=HIGHEST)

    def first_chunk(k):
        rows = pl.ds(k * chunk, chunk)
        both = jnp.concatenate([k_hi[rows, :block], k_lo[rows, :block]], axis=1)
        result = dot(both, w_first[...])
        out1[rows, :] = result[:, :block] + result[:, block:]
        if k % group == group - 1:
            store1(k // group).start()

    second = inverse_factor(schur, first_chunk)
    mixed = -dot(second, carried, precision=HIGHEST)
    high, low = halves(jnp.concatenate([mixed, second], axis=1).T)
    w_hi[...] = jnp.concatenate([high, low], axis=1)
    w_lo[...] = high

    def second_chunk(k, carry):
        rows = pl.ds(pl.multiple_of(k * chunk, chunk), chunk)
        wide = dot(k_hi[rows, :], w_hi[...])
        result = wide[:, :block] + wide[:, block:] + dot(k_lo[rows, :], w_lo[...])
        out2[rows, :] = result
        store2(k).start()
        before = out1[rows, :]
        squares = before * before + result * result
        residual[k] = 1.0 - jnp.sum(squares.T, axis=0, keepdims=True)
        return carry

    lax.fori_loop(0, chunks, second_chunk, 0, unroll=4)
    for k in range(chunks // group):
        store1(k).wait()

    def finish(k, carry):
        store2(k).wait()
        return carry

    lax.fori_loop(0, chunks, finish, 0)


def shards(mesh, frames, pivots):
    points = gather_points(mesh, frames, pivots)
    row_count, feat = frames.shape
    slots = points.shape[0]
    block = slots // 2
    chunks = block // SUB
    vmem = pl.BlockSpec(memory_space=pltpu.VMEM)
    anywhere = pl.BlockSpec(memory_space=pl.ANY)
    factor, residual = pl.pallas_call(
        factor_kernel,
        out_shape=(
            jax.ShapeDtypeStruct((row_count, slots), jnp.float32),
            jax.ShapeDtypeStruct((chunks, 1, row_count // chunks), jnp.float32),
        ),
        in_specs=[vmem, anywhere],
        out_specs=(anywhere, vmem),
        scratch_shapes=[
            pltpu.VMEM((row_count, feat), jnp.float32),
            pltpu.VMEM((4 * feat, slots), jnp.bfloat16),
            pltpu.VMEM((row_count, slots), jnp.bfloat16),
            pltpu.VMEM((row_count, slots), jnp.bfloat16),
            pltpu.VMEM((row_count, block), jnp.float32),
            pltpu.VMEM((row_count, block), jnp.float32),
            pltpu.VMEM((slots, slots), jnp.bfloat16),
            pltpu.VMEM((slots, slots), jnp.bfloat16),
            pltpu.VMEM((slots, block), jnp.bfloat16),
            pltpu.SemaphoreType.DMA((2,)),
            pltpu.SemaphoreType.DMA((4,)),
            pltpu.SemaphoreType.DMA((chunks,)),
        ],
        compiler_params=pltpu.CompilerParams(vmem_limit_bytes=60 * 1024 * 1024),
    )(points, frames)
    return factor, residual.reshape(row_count)


def solution(mesh):
    placed = (P(("groups", "dp", "feat"), None), P("groups", None))
    return jax.shard_map(
        functools.partial(shards, mesh),
        mesh=mesh,
        in_specs=placed,
        out_specs=(P(("groups", "dp", "feat"), None), P(("groups", "dp", "feat"))),
        check_vma=False,
    )
```
